32 devices in a mesh: ctx: 4 (over z), seq: 2 (over x), wa: 4 (over y, core).
Axes of the slice: x: 2, y: 2, z: 4, core: 2. Of those that a mesh axis runs over, the one named last changes fastest.
Arguments:
- tokens: bfloat16 [8, 768, 4096], P('seq', 'wa', 'ctx'), may hold values from -6 to 6
- first_gain: bfloat16 [768], P('wa'), may hold values from 0.5 to 1.5
- qkv_weight: bfloat16 [3, 768, 768], P(None, 'wa'), may hold values from -0.21875 to 0.21875
- attn_out_weight: bfloat16 [768, 768], P('wa'), may hold values from -6 to 6
- second_gain: bfloat16 [768], P('wa'), may hold values from 0.5 to 1.5
- ffn_in_weight: bfloat16 [2, 1152, 768], P(None, 'wa'), may hold values from -0.21875 to 0.21875
- ffn_out_weight: bfloat16 [1152, 768], P('wa'), may hold values from -0.1875 to 0.1875
- cotangent: bfloat16 [8, 768, 4096], P('seq', 'wa', 'ctx'), may hold values from -6 to 6
Outputs:
- output: bfloat16 [8, 768, 4096], P('seq', 'wa', 'ctx')
- grad_tokens: float32 [8, 768, 4096], P('seq', 'wa', 'ctx')
- grad_first_gain: float32 [768], P('wa')
- grad_qkv: float32 [3, 768, 768], P(None, 'wa')
- grad_attn_out: float32 [768, 768], P('wa')
- grad_second_gain: float32 [768], P('wa')
- grad_ffn_in: float32 [2, 1152, 768], P(None, 'wa')
- grad_ffn_out: float32 [1152, 768], P('wa')
The draws below stay inside these ranges and needn't reach their ends.
All inputs are finite; a program needn't handle non-finite values.
Results may differ from the reference program's by a relative error of at most 0.023.
Values may be sent and summed in bfloat16 or wider, within the bound.
A program may use at most 320 MiB of HBM per device.

```python
import math
import jax
import jax.numpy as jnp
from jax import lax

D = 768
HEADS = 12
HD = 64
FF = 1152
SEQ_LEN = 4096
SEQS = 8


def block_scale(key, extent, pieces, least, high):
    loudness = 1.0
    for dim, shards_of in pieces:
        steps = jax.random.uniform(jax.random.fold_in(jax.random.fold_in(key, 6), dim), (shards_of,), jnp.float32, least / len(pieces), high / len(pieces))
        loudness = loudness * jnp.repeat(jnp.exp(steps), extent[dim] // shards_of).reshape((-1,) + (1,) * (len(extent) - 1 - dim))
    return loudness


def noise(own_key, dims, width, limit, cuts=(), kind=jnp.bfloat16):
    values = width * jax.random.normal(own_key, dims, jnp.float32)
    if cuts:
        values = values * block_scale(own_key, dims, cuts, -0.22, 0.18)
    return jnp.clip(values, -limit, limit).astype(kind)


def setup_inputs(seed: int = 0) -> dict:
    arg_keys = jax.random.split(jax.random.key(seed), 9)
    tokens = noise(arg_keys[0], (SEQS, D, SEQ_LEN), 1.0, 6.0, ((0, 2), (1, 4), (2, 4)))
    first_gain = jnp.clip(1.0 + 0.1 * jax.random.normal(arg_keys[1], (D,), jnp.float32), 0.5, 1.5).astype(jnp.bfloat16)
    qkv_weight = noise(arg_keys[2], (3, D, D), D ** -0.5, 0.21875, ((1, 4),))
    attn_out_weight = noise(arg_keys[3], (D, D), ((SEQ_LEN // (2 * D) + 1) ** 0.5), 6.0, ((0, 4),))
    second_gain = jnp.clip(1.0 + 0.1 * jax.random.normal(arg_keys[4], (D,), jnp.float32), 0.5, 1.5).astype(jnp.bfloat16)
    ffn_in_weight = noise(arg_keys[5], (2, FF, D), D ** -0.5, 0.21875, ((1, 4),))
    ffn_out_weight = noise(arg_keys[6], (FF, D), FF ** -0.5, 0.1875, ((0, 4),))
    cotangent = noise(arg_keys[7], (SEQS, D, SEQ_LEN), 1.0, 6.0, ((0, 2), (1, 4), (2, 4)))
    return dict(tokens=tokens, first_gain=first_gain, qkv_weight=qkv_weight, attn_out_weight=attn_out_weight, second_gain=second_gain, ffn_in_weight=ffn_in_weight, ffn_out_weight=ffn_out_weight, cotangent=cotangent)


EPSILON = 1e-05
THETA_BASE = 160000.0
HIGHEST = lax.Precision.HIGHEST

@jax.custom_vjp
def low(v):
    return lax.optimization_barrier(v.astype(jnp.bfloat16)).astype(jnp.float32)

@jax.custom_vjp
def low_back(v):
    return v

def low_keep(v):
    return (low(v), None)

def low_pass(kept, grad):
    return (grad,)

def back_keep(v):
    return (v, None)

def back_low(kept, grad):
    return (low(grad),)
low.defvjp(low_keep, low_pass)
low_back.defvjp(back_keep, back_low)

def rope_tables(positions, head_size):
    half_size = head_size // 2
    frequency = THETA_BASE ** (-jnp.arange(half_size, dtype=jnp.float32) * 2.0 / head_size)
    angles = positions.astype(jnp.float32)[:, None] * frequency[None, :]
    return (jnp.cos(angles)[:, None, :], jnp.sin(angles)[:, None, :])

def rotate(values, cosine_table, sine_table):
    half_size = values.shape[-1] // 2
    first_half = values[..., :half_size]
    second_half = values[..., half_size:]
    return jnp.concatenate([first_half * cosine_table - second_half * sine_table, second_half * cosine_table + first_half * sine_table], axis=-1)

def normalize_rows(rows_in, gain_vec):
    center = rows_in - lax.optimization_barrier(jnp.mean(rows_in, axis=-1, keepdims=True))
    spread = lax.optimization_barrier(jnp.mean(center * center, axis=-1, keepdims=True))
    return center * lax.rsqrt(spread + EPSILON) * gain_vec

def layer_forward(inputs, gain_one, qkv_mat, attn_mat, gain_two, ffn_in_mat, ffn_out_mat):
    length = inputs.shape[0]
    cosine_table, sine_table = rope_tables(jnp.arange(length, dtype=jnp.int32), HD)
    normed_one = low(normalize_rows(inputs, gain_one))
    projected = low_back(jnp.einsum('td,kfd->tkf', normed_one, qkv_mat, precision=HIGHEST))
    projected = projected.reshape(length, 3, HEADS, HD)
    queries = low(rotate(projected[:, 0], cosine_table, sine_table))
    keys_all = low(rotate(projected[:, 1], cosine_table, sine_table))
    values_all = low(projected[:, 2])
    score_scale = 1.0 / math.sqrt(HD)
    query_rows = math.gcd(length, 512)

    def attend_block(query_part):
        scores = low_back(jnp.einsum('qhe,khe->hqk', query_part, keys_all, precision=HIGHEST) * score_scale)
        row_max = lax.optimization_barrier(jnp.max(scores, axis=-1, keepdims=True))
        weights = jnp.exp(scores - row_max)
        prob_rows = low(weights / lax.optimization_barrier(jnp.sum(weights, axis=-1, keepdims=True)))
        return jnp.einsum('hqk,khe->qhe', prob_rows, values_all, precision=HIGHEST)
    attended = lax.map(jax.checkpoint(attend_block), queries.reshape(length // query_rows, query_rows, HEADS, HD))
    attended = low_back(low(attended.reshape(length, HEADS * HD)))
    middle = inputs + low_back(jnp.dot(attended, attn_mat, precision=HIGHEST))
    normed_two = low(normalize_rows(middle, gain_two))
    gate_up = jnp.einsum('td,kfd->tkf', normed_two, ffn_in_mat, precision=HIGHEST)
    gate_part = low_back(gate_up[:, 0])
    up_part = low_back(gate_up[:, 1])
    hidden = low(jax.nn.gelu(gate_part, approximate=False) * up_part)
    return middle + low_back(jnp.dot(hidden, ffn_out_mat, precision=HIGHEST))

def reference(tokens, first_gain, qkv_weight, attn_out_weight, second_gain, ffn_in_weight, ffn_out_weight, cotangent):
    gain_one = first_gain.astype(jnp.float32)
    qkv_mat = qkv_weight.astype(jnp.float32)
    attn_mat = attn_out_weight.astype(jnp.float32)
    gain_two = second_gain.astype(jnp.float32)
    ffn_in_mat = ffn_in_weight.astype(jnp.float32)
    ffn_out_mat = ffn_out_weight.astype(jnp.float32)

    def per_sequence(totals, items):
        seq_tokens, seq_cot = items
        rows_in = seq_tokens.astype(jnp.float32).T
        result, pull_back = jax.vjp(layer_forward, rows_in, gain_one, qkv_mat, attn_mat, gain_two, ffn_in_mat, ffn_out_mat)
        gradients = pull_back(seq_cot.astype(jnp.float32).T)
        new_totals = tuple((summed + gradient for summed, gradient in zip(totals, gradients[1:])))
        return (new_totals, (result.T.astype(jnp.bfloat16), gradients[0].T))
    start_totals = (jnp.zeros_like(gain_one), jnp.zeros_like(qkv_mat), jnp.zeros_like(attn_mat), jnp.zeros_like(gain_two), jnp.zeros_like(ffn_in_mat), jnp.zeros_like(ffn_out_mat))
    totals, (output, grad_tokens) = lax.scan(per_sequence, start_totals, (tokens, cotangent))
    return (output, grad_tokens, totals[0], totals[1], totals[2], totals[3], totals[4], totals[5])
```

```python
import functools
import math

import jax
import jax.numpy as jnp
from jax import lax
from jax.experimental import pallas as pl
from jax.experimental.pallas import tpu as pltpu
from jax.sharding import PartitionSpec as P

HD = 64
EPSILON = 1e-05
THETA_BASE = 160000.0
GROUPS = 3
LOG2E = math.log2(math.e)
F32 = jnp.float32
BF16 = jnp.bfloat16


def dot(a, b, contract_a, contract_b):
    return lax.dot_general(
        a, b, (((contract_a,), (contract_b,)), ((), ())), preferred_element_type=F32
    )


def rope_tables(positions, head_size):
    half_size = head_size // 2
    frequency = THETA_BASE ** (-jnp.arange(half_size, dtype=F32) * 2.0 / head_size)
    angles = frequency[:, None] * positions.astype(F32)[None, :]
    return (jnp.cos(angles), jnp.sin(angles))


def rotate(values, cosine_table, sine_table):
    half_size = values.shape[1] // 2
    first_half = values[:, :half_size]
    second_half = values[:, half_size:]
    return jnp.concatenate(
        [
            first_half * cosine_table - second_half * sine_table,
            second_half * cosine_table + first_half * sine_table,
        ],
        axis=1,
    )


def normalize(columns_in):
    center = columns_in - jnp.mean(columns_in, axis=0, keepdims=True)
    inverse = lax.rsqrt(jnp.mean(center * center, axis=0, keepdims=True) + EPSILON)
    return (center * inverse, inverse)


def norm_back(grad_hat, normed_hat, inverse):
    mean_grad = jnp.mean(grad_hat, axis=0, keepdims=True)
    mean_proj = jnp.mean(grad_hat * normed_hat, axis=0, keepdims=True)
    return inverse * (grad_hat - mean_grad - normed_hat * mean_proj)


def forward_kernel(q_ref, kv_ref, out_ref, lse_ref, acc_ref, max_ref, *, key_tile):
    queries = q_ref[0]
    blocks, length = kv_ref.shape[0], kv_ref.shape[4]
    acc_ref[...] = jnp.zeros_like(acc_ref)
    max_ref[...] = jnp.full_like(max_ref, -jnp.inf)

    def block_step(block, carry):
        for start in range(0, length, key_tile):
            keys = kv_ref[block, 0, 0, :, pl.ds(start, key_tile)]
            values = kv_ref[block, 1, 0, :, pl.ds(start, key_tile)]
            scores = dot(keys, queries, 0, 0)
            old_max = max_ref[...]
            new_max = jnp.maximum(old_max, jnp.max(scores, axis=0, keepdims=True))
            weights = jnp.exp2(scores - new_max).astype(BF16)
            values_ones = jnp.concatenate([values, jnp.ones((16, key_tile), BF16)], axis=0)
            acc_ref[...] = acc_ref[...] * jnp.exp2(old_max - new_max) + dot(
                values_ones, weights, 1, 0
            )
            max_ref[...] = new_max
        return carry

    lax.fori_loop(0, blocks, block_step, 0)
    total = acc_ref[HD : HD + 1, :]
    out_ref[0] = acc_ref[:HD, :] / total
    lse_ref[0] = max_ref[...] + jnp.log2(total)


def attend(queries, kv_all):
    heads, head_size, length = queries.shape
    blocks, key_length = kv_all.shape[0], kv_all.shape[4]
    pairs = heads * length * blocks * key_length
    return pl.pallas_call(
        functools.partial(forward_kernel, key_tile=math.gcd(key_length, 512)),
        grid=(heads,),
        in_specs=[
            pl.BlockSpec((1, head_size, length), lambda h: (h, 0, 0)),
            pl.BlockSpec((blocks, 2, 1, head_size, key_length), lambda h: (0, 0, h, 0, 0)),
        ],
        out_specs=[
            pl.BlockSpec((1, head_size, length), lambda h: (h, 0, 0)),
            pl.BlockSpec((1, 1, length), lambda h: (h, 0, 0)),
        ],
        out_shape=[
            jax.ShapeDtypeStruct((heads, head_size, length), F32),
            jax.ShapeDtypeStruct((heads, 1, length), F32),
        ],
        scratch_shapes=[pltpu.VMEM((head_size + 16, length), F32), pltpu.VMEM((1, length), F32)],
        compiler_params=pltpu.CompilerParams(vmem_limit_bytes=48 * 1024 * 1024),
        cost_estimate=pl.CostEstimate(
            flops=16 * pairs * head_size, bytes_accessed=4 * kv_all.size, transcendentals=pairs
        ),
    )(queries, kv_all)


def split_rows(row, count):
    high = row.astype(BF16).astype(F32)
    middle = (row - high).astype(BF16).astype(F32)
    least = row - high - middle
    index = lax.broadcasted_iota(jnp.int32, (count, row.shape[1]), 0)
    stacked = jnp.where(
        index == 0, high, jnp.where(index == 1, middle, jnp.where(index == 2, least, 0.0))
    )
    return stacked.astype(BF16)


def backward_kernel(q_ref, kv_ref, go_ref, out_ref, lse_ref, gq_ref, gkv_ref, *, key_tile):
    queries = q_ref[0]
    grad_out = go_ref[0]
    blocks, length = kv_ref.shape[0], kv_ref.shape[4]
    grad_dot = jnp.sum(grad_out.astype(F32) * out_ref[0], axis=0, keepdims=True)
    queries_more = jnp.concatenate([queries, split_rows(lse_ref[0], 16)], axis=0)
    grad_more = jnp.concatenate([grad_out, split_rows(grad_dot, 16)], axis=0)
    index = lax.broadcasted_iota(jnp.int32, (16, key_tile), 0)
    minus = jnp.where(index < 3, -1.0, 0.0).astype(BF16)
    gq_ref[...] = jnp.zeros_like(gq_ref)

    def block_step(block, carry):
        for start in range(0, length, key_tile):
            keys = kv_ref[block, 0, 0, :, pl.ds(start, key_tile)]
            values = kv_ref[block, 1, 0, :, pl.ds(start, key_tile)]
            probs = jnp.exp2(dot(jnp.concatenate([keys, minus], axis=0), queries_more, 0, 0))
            grad_probs = dot(jnp.concatenate([values, minus], axis=0), grad_more, 0, 0)
            grad_scores = (probs * grad_probs).astype(BF16)
            gq_ref[0] += dot(keys, grad_scores, 1, 0)
            grad_keys = dot(queries, grad_scores, 1, 1) * (1.0 / LOG2E)
            grad_values = dot(grad_out, probs.astype(BF16), 1, 1)
            gkv_ref[block, 0, 0, :, pl.ds(start, key_tile)] = grad_keys.astype(BF16)
            gkv_ref[block, 1, 0, :, pl.ds(start, key_tile)] = grad_values.astype(BF16)
        return carry

    lax.fori_loop(0, blocks, block_step, 0)


def attend_back(queries, kv_all, grad_out, out, lse):
    heads, head_size, length = queries.shape
    blocks, key_length = kv_all.shape[0], kv_all.shape[4]
    pairs = heads * length * blocks * key_length
    per_head = pl.BlockSpec((1, head_size, length), lambda h: (h, 0, 0))
    per_kv = pl.BlockSpec((blocks, 2, 1, head_size, key_length), lambda h: (0, 0, h, 0, 0))
    return pl.pallas_call(
        functools.partial(backward_kernel, key_tile=math.gcd(key_length, 512)),
        grid=(heads,),
        in_specs=[
            per_head,
            per_kv,
            per_head,
            per_head,
            pl.BlockSpec((1, 1, length), lambda h: (h, 0, 0)),
        ],
        out_specs=[per_head, per_kv],
        out_shape=[
            jax.ShapeDtypeStruct((heads, head_size, length), F32),
            jax.ShapeDtypeStruct(kv_all.shape, BF16),
        ],
        compiler_params=pltpu.CompilerParams(vmem_limit_bytes=48 * 1024 * 1024),
        cost_estimate=pl.CostEstimate(
            flops=40 * pairs * head_size, bytes_accessed=8 * kv_all.size, transcendentals=pairs
        ),
    )(queries, kv_all, grad_out, out, lse)


def local(
    tokens,
    first_gain,
    qkv_weight,
    attn_out_weight,
    second_gain,
    ffn_in_weight,
    ffn_out_weight,
    cotangent,
):
    wa_size = lax.axis_size("wa")
    length = tokens.shape[2]
    width = qkv_weight.shape[2]
    shard = qkv_weight.shape[1]
    hidden_shard = ffn_in_weight.shape[1]
    heads = width // HD
    assert tokens.shape[0] == wa_size
    per_group = heads // GROUPS
    score_scale = 1.0 / math.sqrt(HD)

    x_low = lax.all_to_all(tokens, "wa", 0, 1, tiled=True)[0]
    qkv_all = lax.all_gather(qkv_weight, "wa", axis=0)
    gains = lax.all_gather(jnp.stack([first_gain, second_gain]), "wa", axis=0)
    gains = gains.transpose(1, 0, 2).reshape(2, width, 1).astype(F32)
    gain_one, gain_two = gains[0], gains[1]
    cot = lax.all_to_all(cotangent, "wa", 0, 1, tiled=True)[0]
    attn_mat = lax.all_gather(attn_out_weight, "wa", axis=0).reshape(width, width)
    ffn_in_mat = lax.all_gather(ffn_in_weight, "wa", axis=0).reshape(-1, width)
    ffn_out_mat = lax.all_gather(ffn_out_weight, "wa", axis=0).reshape(-1, width)
    qkv_mat = qkv_all.reshape(-1, width)

    x = x_low.astype(F32)
    hat_one, inv_one = normalize(x)
    normed_one = (hat_one * gain_one).astype(BF16)
    projected = dot(qkv_mat, normed_one, 1, 0).reshape(wa_size, 3, shard, length)
    positions = lax.axis_index("ctx") * length + jnp.arange(length, dtype=jnp.int32)
    cosine_table, sine_table = rope_tables(positions, HD)

    def by_head(index):
        return projected[:, index].reshape(heads, HD, length)

    queries = rotate(
        by_head(0), cosine_table * (score_scale * LOG2E), sine_table * (score_scale * LOG2E)
    ).astype(BF16)
    keys_own = rotate(by_head(1), cosine_table, sine_table).astype(BF16)
    values_own = by_head(2).astype(BF16)

    parts = []
    for group in range(GROUPS):
        rows = slice(group * per_group, (group + 1) * per_group)
        kv_all = lax.all_gather(jnp.stack([keys_own[rows], values_own[rows]]), "ctx", axis=0)
        parts.append((rows, kv_all))
    results = [attend(queries[rows], kv_all) for rows, kv_all in parts]
    attended_low = jnp.concatenate([r[0].astype(BF16) for r in results], axis=0).reshape(
        width, length
    )
    middle = x + dot(attn_mat, attended_low, 0, 0)
    hat_two, inv_two = normalize(middle)
    normed_two = (hat_two * gain_two).astype(BF16)
    gate_up = dot(ffn_in_mat, normed_two, 1, 0).reshape(wa_size, 2, hidden_shard, length)
    gate, up = gate_up[:, 0], gate_up[:, 1]
    cdf = 0.5 * (1.0 + lax.erf(gate * math.sqrt(0.5)))
    gelu = gate * cdf
    hidden = (gelu * up).astype(BF16).reshape(-1, length)
    output_all = (middle + dot(ffn_out_mat, hidden, 0, 0)).astype(BF16)
    output = lax.all_to_all(output_all[None], "wa", 1, 0, tiled=True)

    grad_ffn_out = dot(hidden, cot, 1, 1)
    grad_hidden = dot(ffn_out_mat, cot, 1, 0).reshape(gate.shape)
    slope = cdf + gate * (jnp.exp(-0.5 * gate * gate) * (1.0 / math.sqrt(2.0 * math.pi)))
    grad_gate_up = (
        jnp.stack([grad_hidden * up * slope, grad_hidden * gelu], axis=1)
        .astype(BF16)
        .reshape(-1, length)
    )
    grad_ffn_in = dot(grad_gate_up, normed_two, 1, 1)
    grad_normed_two = dot(ffn_in_mat, grad_gate_up, 0, 0)
    gain_two_grad = jnp.sum(grad_normed_two * hat_two, axis=1)
    grad_middle = cot.astype(F32) + norm_back(grad_normed_two * gain_two, hat_two, inv_two)
    grad_middle_low = grad_middle.astype(BF16)
    grad_attn_out = dot(attended_low, grad_middle_low, 1, 1)
    grad_attended = dot(attn_mat, grad_middle_low, 1, 0).astype(BF16).reshape(heads, HD, length)

    def sum_weights(grads):
        own = lax.psum_scatter(grads.astype(BF16), "wa", scatter_dimension=0)
        return lax.psum(own, ("ctx", "seq")).astype(F32)

    early = sum_weights(
        jnp.concatenate(
            [
                grad_ffn_in.astype(BF16).reshape(wa_size, -1, width),
                grad_ffn_out.astype(BF16).reshape(wa_size, -1, width),
                grad_attn_out.astype(BF16).reshape(wa_size, -1, width),
            ],
            axis=1,
        )
    )
    grad_ffn_in_own = early[: 2 * hidden_shard].reshape(2, hidden_shard, width)
    grad_ffn_out_own = early[2 * hidden_shard : 3 * hidden_shard]
    grad_attn_out_own = early[3 * hidden_shard :]

    grad_queries, grad_kv = [], []
    for (rows, kv_all), (out, lse) in zip(parts, results):
        grad_q, grad_kv_all = attend_back(queries[rows], kv_all, grad_attended[rows], out, lse)
        grad_queries.append(grad_q)
        grad_kv.append(lax.psum_scatter(grad_kv_all, "ctx", scatter_dimension=0))
    grad_q = jnp.concatenate(grad_queries, axis=0)
    grad_k = jnp.concatenate([g[0] for g in grad_kv], axis=0).astype(F32)
    grad_v = jnp.concatenate([g[1] for g in grad_kv], axis=0)
    grad_q = rotate(grad_q, cosine_table * score_scale, -sine_table * score_scale).astype(BF16)
    grad_k = rotate(grad_k, cosine_table, -sine_table).astype(BF16)
    grad_projected = jnp.stack(
        [g.reshape(wa_size, shard, length) for g in (grad_q, grad_k, grad_v)], axis=1
    ).reshape(-1, length)
    grad_normed_one = dot(qkv_mat, grad_projected, 0, 0)
    gain_one_grad = jnp.sum(grad_normed_one * hat_one, axis=1)
    grad_x = grad_middle + norm_back(grad_normed_one * gain_one, hat_one, inv_one)
    grad_tokens = lax.all_to_all(grad_x.astype(BF16)[None], "wa", 1, 0, tiled=True).astype(F32)
    grad_qkv = dot(grad_projected, normed_one, 1, 1)
    grad_qkv_own = sum_weights(grad_qkv.reshape(wa_size, -1, width)).reshape(3, shard, width)
    gain_sums = lax.psum(jnp.stack([gain_one_grad, gain_two_grad]), ("ctx", "seq", "wa"))
    gain_own = lax.dynamic_slice_in_dim(gain_sums, lax.axis_index("wa") * shard, shard, 1)
    return (
        output,
        grad_tokens,
        gain_own[0],
        grad_qkv_own,
        grad_attn_out_own,
        gain_own[1],
        grad_ffn_in_own,
        grad_ffn_out_own,
    )


def solution(mesh):
    return jax.shard_map(
        local,
        mesh=mesh,
        in_specs=(
            P("seq", "wa", "ctx"),
            P("wa"),
            P(None, "wa", None),
            P("wa", None),
            P("wa"),
            P(None, "wa", None),
            P("wa", None),
            P("seq", "wa", "ctx"),
        ),
        out_specs=(
            P("seq", "wa", "ctx"),
            P("seq", "wa", "ctx"),
            P("wa"),
            P(None, "wa", None),
            P("wa", None),
            P("wa"),
            P(None, "wa", None),
            P("wa", None),
        ),
        check_vma=False,
    )
```

```python
import functools
import math

import jax
import jax.numpy as jnp
from jax import lax
from jax.experimental import pallas as pl
from jax.experimental.pallas import tpu as pltpu
from jax.sharding import PartitionSpec as P

HD = 64
EPSILON = 1e-05
THETA_BASE = 160000.0
LOG2E = math.log2(math.e)
F32 = jnp.float32
BF16 = jnp.bfloat16


def dot(a, b, contract_a, contract_b):
    return lax.dot_general(
        a, b, (((contract_a,), (contract_b,)), ((), ())), preferred_element_type=F32
    )


def rope_tables(positions, head_size):
    half_size = head_size // 2
    frequency = THETA_BASE ** (-jnp.arange(half_size, dtype=F32) * 2.0 / head_size)
    angles = frequency[:, None] * positions.astype(F32)[None, :]
    return (jnp.cos(angles), jnp.sin(angles))


def rotate(values, cosine_table, sine_table):
    half_size = values.shape[1] // 2
    first_half = values[:, :half_size]
    second_half = values[:, half_size:]
    return jnp.concatenate(
        [
            first_half * cosine_table - second_half * sine_table,
            second_half * cosine_table + first_half * sine_table,
        ],
        axis=1,
    )


def normalize(columns_in):
    center = columns_in - jnp.mean(columns_in, axis=0, keepdims=True)
    inverse = lax.rsqrt(jnp.mean(center * center, axis=0, keepdims=True) + EPSILON)
    return (center * inverse, inverse)


def norm_back(grad_hat, normed_hat, inverse):
    mean_grad = jnp.mean(grad_hat, axis=0, keepdims=True)
    mean_proj = jnp.mean(grad_hat * normed_hat, axis=0, keepdims=True)
    return inverse * (grad_hat - mean_grad - normed_hat * mean_proj)


def forward_kernel(q_ref, kv_ref, out_ref, lse_ref, acc_ref, max_ref, *, key_tile):
    queries = q_ref[0]
    blocks, length = kv_ref.shape[0], kv_ref.shape[4]
    acc_ref[...] = jnp.zeros_like(acc_ref)
    max_ref[...] = jnp.full_like(max_ref, -jnp.inf)

    def block_step(block, carry):
        for start in range(0, length, key_tile):
            keys = kv_ref[block, 0, 0, :, pl.ds(start, key_tile)]
            values = kv_ref[block, 1, 0, :, pl.ds(start, key_tile)]
            scores = dot(keys, queries, 0, 0)
            old_max = max_ref[...]
            new_max = jnp.maximum(old_max, jnp.max(scores, axis=0, keepdims=True))
            weights = jnp.exp2(scores - new_max).astype(BF16)
            values_ones = jnp.concatenate([values, jnp.ones((16, key_tile), BF16)], axis=0)
            acc_ref[...] = acc_ref[...] * jnp.exp2(old_max - new_max) + dot(
                values_ones, weights, 1, 0
            )
            max_ref[...] = new_max
        return carry

    lax.fori_loop(0, blocks, block_step, 0)
    total = acc_ref[HD : HD + 1, :]
    out_ref[0] = acc_ref[:HD, :] / total
    lse_ref[0] = max_ref[...] + jnp.log2(total)


def attend(queries, kv_all):
    heads, head_size, length = queries.shape
    blocks, key_length = kv_all.shape[0], kv_all.shape[4]
    pairs = heads * length * blocks * key_length
    return pl.pallas_call(
        functools.partial(forward_kernel, key_tile=math.gcd(key_length, 512)),
        grid=(heads,),
        in_specs=[
            pl.BlockSpec((1, head_size, length), lambda h: (h, 0, 0)),
            pl.BlockSpec((blocks, 2, 1, head_size, key_length), lambda h: (0, 0, h, 0, 0)),
        ],
        out_specs=[
            pl.BlockSpec((1, head_size, length), lambda h: (h, 0, 0)),
            pl.BlockSpec((1, 1, length), lambda h: (h, 0, 0)),
        ],
        out_shape=[
            jax.ShapeDtypeStruct((heads, head_size, length), F32),
            jax.ShapeDtypeStruct((heads, 1, length), F32),
        ],
        scratch_shapes=[pltpu.VMEM((head_size + 16, length), F32), pltpu.VMEM((1, length), F32)],
        compiler_params=pltpu.CompilerParams(vmem_limit_bytes=48 * 1024 * 1024),
        cost_estimate=pl.CostEstimate(
            flops=16 * pairs * head_size, bytes_accessed=4 * kv_all.size, transcendentals=pairs
        ),
    )(queries, kv_all)


def split_rows(row, count):
    high = row.astype(BF16).astype(F32)
    middle = (row - high).astype(BF16).astype(F32)
    least = row - high - middle
    index = lax.broadcasted_iota(jnp.int32, (count, row.shape[1]), 0)
    stacked = jnp.where(
        index == 0, high, jnp.where(index == 1, middle, jnp.where(index == 2, least, 0.0))
    )
    return stacked.astype(BF16)


def backward_kernel(q_ref, kv_ref, go_ref, out_ref, lse_ref, gq_ref, gkv_ref, *, key_tile):
    queries = q_ref[0]
    grad_out = go_ref[0]
    blocks, length = kv_ref.shape[0], kv_ref.shape[4]
    grad_dot = jnp.sum(grad_out.astype(F32) * out_ref[0], axis=0, keepdims=True)
    queries_more = jnp.concatenate([queries, split_rows(lse_ref[0], 16)], axis=0)
    grad_more = jnp.concatenate([grad_out, split_rows(grad_dot, 16)], axis=0)
    index = lax.broadcasted_iota(jnp.int32, (16, key_tile), 0)
    minus = jnp.where(index < 3, -1.0, 0.0).astype(BF16)
    gq_ref[...] = jnp.zeros_like(gq_ref)

    def block_step(block, carry):
        for start in range(0, length, key_tile):
            keys = kv_ref[block, 0, 0, :, pl.ds(start, key_tile)]
            values = kv_ref[block, 1, 0, :, pl.ds(start, key_tile)]
            probs = jnp.exp2(dot(jnp.concatenate([keys, minus], axis=0), queries_more, 0, 0))
            grad_probs = dot(jnp.concatenate([values, minus], axis=0), grad_more, 0, 0)
            grad_scores = (probs * grad_probs).astype(BF16)
            gq_ref[0] += dot(keys, grad_scores, 1, 0)
            grad_keys = dot(queries, grad_scores, 1, 1) * (1.0 / LOG2E)
            grad_values = dot(grad_out, probs.astype(BF16), 1, 1)
            gkv_ref[block, 0, 0, :, pl.ds(start, key_tile)] = grad_keys.astype(BF16)
            gkv_ref[block, 1, 0, :, pl.ds(start, key_tile)] = grad_values.astype(BF16)
        return carry

    lax.fori_loop(0, blocks, block_step, 0)


def attend_back(queries, kv_all, grad_out, out, lse):
    heads, head_size, length = queries.shape
    blocks, key_length = kv_all.shape[0], kv_all.shape[4]
    pairs = heads * length * blocks * key_length
    per_head = pl.BlockSpec((1, head_size, length), lambda h: (h, 0, 0))
    per_kv = pl.BlockSpec((blocks, 2, 1, head_size, key_length), lambda h: (0, 0, h, 0, 0))
    return pl.pallas_call(
        functools.partial(backward_kernel, key_tile=math.gcd(key_length, 512)),
        grid=(heads,),
        in_specs=[
            per_head,
            per_kv,
            per_head,
            per_head,
            pl.BlockSpec((1, 1, length), lambda h: (h, 0, 0)),
        ],
        out_specs=[per_head, per_kv],
        out_shape=[
            jax.ShapeDtypeStruct((heads, head_size, length), F32),
            jax.ShapeDtypeStruct(kv_all.shape, BF16),
        ],
        compiler_params=pltpu.CompilerParams(vmem_limit_bytes=48 * 1024 * 1024),
        cost_estimate=pl.CostEstimate(
            flops=40 * pairs * head_size, bytes_accessed=8 * kv_all.size, transcendentals=pairs
        ),
    )(queries, kv_all, grad_out, out, lse)


def local(
    tokens,
    first_gain,
    qkv_weight,
    attn_out_weight,
    second_gain,
    ffn_in_weight,
    ffn_out_weight,
    cotangent,
):
    wa_size = lax.axis_size("wa")
    length = tokens.shape[2]
    width = qkv_weight.shape[2]
    shard = qkv_weight.shape[1]
    hidden_shard = ffn_in_weight.shape[1]
    heads = width // HD
    assert tokens.shape[0] == wa_size
    group_sizes = (heads // 3, heads // 4, heads // 4)
    group_sizes += (heads - sum(group_sizes),)
    score_scale = 1.0 / math.sqrt(HD)

    x_low = lax.all_to_all(tokens, "wa", 0, 0, tiled=True).reshape(width, length)
    qkv_all = lax.all_gather(qkv_weight, "wa", axis=0)
    gains = lax.all_gather(jnp.stack([first_gain, second_gain]), "wa", axis=0)
    gains = gains.transpose(1, 0, 2).reshape(2, width, 1).astype(F32)
    gain_one, gain_two = gains[0], gains[1]
    cot = lax.all_to_all(cotangent, "wa", 0, 0, tiled=True).reshape(width, length)
    attn_mat = lax.all_gather(attn_out_weight, "wa", axis=0).reshape(width, width)
    ffn_in_mat = lax.all_gather(ffn_in_weight, "wa", axis=0).reshape(-1, width)
    ffn_out_mat = lax.all_gather(ffn_out_weight, "wa", axis=0).reshape(-1, width)
    qkv_mat = qkv_all.reshape(-1, width)

    x = x_low.astype(F32)
    hat_one, inv_one = normalize(x)
    normed_one = (hat_one * gain_one).astype(BF16)
    projected = dot(qkv_mat, normed_one, 1, 0).reshape(wa_size, 3, shard, length)
    positions = lax.axis_index("ctx") * length + jnp.arange(length, dtype=jnp.int32)
    cosine_table, sine_table = rope_tables(positions, HD)

    def by_head(index):
        return projected[:, index].reshape(heads, HD, length)

    queries = rotate(
        by_head(0), cosine_table * (score_scale * LOG2E), sine_table * (score_scale * LOG2E)
    ).astype(BF16)
    keys_own = rotate(by_head(1), cosine_table, sine_table).astype(BF16)
    values_own = by_head(2).astype(BF16)

    parts = []
    for group, size in enumerate(group_sizes):
        first = sum(group_sizes[:group])
        rows = slice(first, first + size)
        kv_all = lax.all_gather(jnp.stack([keys_own[rows], values_own[rows]]), "ctx", axis=0)
        parts.append((rows, kv_all))
    results = [attend(queries[rows], kv_all) for rows, kv_all in parts]
    attended_low = jnp.concatenate([r[0].astype(BF16) for r in results], axis=0).reshape(
        width, length
    )
    middle = x + dot(attn_mat, attended_low, 0, 0)
    hat_two, inv_two = normalize(middle)
    normed_two = (hat_two * gain_two).astype(BF16)
    gate_up = dot(ffn_in_mat, normed_two, 1, 0).reshape(wa_size, 2, hidden_shard, length)
    gate, up = gate_up[:, 0], gate_up[:, 1]
    cdf = 0.5 * (1.0 + lax.erf(gate * math.sqrt(0.5)))
    gelu = gate * cdf
    hidden = (gelu * up).astype(BF16).reshape(-1, length)
    output_all = (middle + dot(ffn_out_mat, hidden, 0, 0)).astype(BF16)
    output = lax.all_to_all(output_all.reshape(tokens.shape), "wa", 0, 0, tiled=True)

    grad_ffn_out = dot(hidden, cot, 1, 1)
    grad_hidden = dot(ffn_out_mat, cot, 1, 0).reshape(gate.shape)
    slope = cdf + gate * (jnp.exp(-0.5 * gate * gate) * (1.0 / math.sqrt(2.0 * math.pi)))
    grad_gate_up = (
        jnp.stack([grad_hidden * up * slope, grad_hidden * gelu], axis=1)
        .astype(BF16)
        .reshape(-1, length)
    )
    grad_ffn_in = dot(grad_gate_up, normed_two, 1, 1)
    grad_normed_two = dot(ffn_in_mat, grad_gate_up, 0, 0)
    gain_two_grad = jnp.sum(grad_normed_two * hat_two, axis=1)
    grad_middle = cot.astype(F32) + norm_back(grad_normed_two * gain_two, hat_two, inv_two)
    grad_middle_low = grad_middle.astype(BF16)
    grad_attn_out = dot(attended_low, grad_middle_low, 1, 1)
    grad_attended = dot(attn_mat, grad_middle_low, 1, 0).astype(BF16).reshape(heads, HD, length)

    early_own = lax.psum_scatter(
        jnp.concatenate(
            [
                grad_ffn_in.astype(BF16).reshape(wa_size, -1, width),
                grad_ffn_out.astype(BF16).reshape(wa_size, -1, width),
                grad_attn_out.astype(BF16).reshape(wa_size, -1, width),
            ],
            axis=1,
        ),
        "wa",
        scatter_dimension=0,
    )
    grad_queries, grad_kv = [], []
    for group in reversed(range(len(parts))):
        (rows, kv_all), (out, lse) = parts[group], results[group]
        grad_part = grad_attended[rows]
        if group == 0:
            grad_part, early = lax.optimization_barrier((grad_part, early))
        grad_q, grad_kv_all = attend_back(queries[rows], kv_all, grad_part, out, lse)
        if group == len(parts) - 1:
            early_own, grad_q = lax.optimization_barrier((early_own, grad_q))
            early = lax.psum(early_own, ("ctx", "seq"))
        grad_queries.append(grad_q)
        grad_kv.append(lax.psum_scatter(grad_kv_all, "ctx", scatter_dimension=0))
    early = early.astype(F32)
    grad_ffn_in_own = early[: 2 * hidden_shard].reshape(2, hidden_shard, width)
    grad_ffn_out_own = early[2 * hidden_shard : 3 * hidden_shard]
    grad_attn_out_own = early[3 * hidden_shard :]
    grad_queries, grad_kv = grad_queries[::-1], grad_kv[::-1]
    grad_q = jnp.concatenate(grad_queries, axis=0)
    grad_k = jnp.concatenate([g[0] for g in grad_kv], axis=0).astype(F32)
    grad_v = jnp.concatenate([g[1] for g in grad_kv], axis=0)
    grad_q = rotate(grad_q, cosine_table * score_scale, -sine_table * score_scale).astype(BF16)
    grad_k = rotate(grad_k, cosine_table, -sine_table).astype(BF16)
    grad_projected = jnp.stack(
        [g.reshape(wa_size, shard, length) for g in (grad_q, grad_k, grad_v)], axis=1
    ).reshape(-1, length)
    grad_normed_one = dot(qkv_mat, grad_projected, 0, 0)
    gain_one_grad = jnp.sum(grad_normed_one * hat_one, axis=1)
    grad_x = grad_middle + norm_back(grad_normed_one * gain_one, hat_one, inv_one)
    grad_tokens = lax.all_to_all(
        grad_x.astype(BF16).reshape(tokens.shape), "wa", 0, 0, tiled=True
    ).astype(F32)
    grad_qkv = dot(grad_projected, normed_one, 1, 1)
    gain_rows = jnp.stack([gain_one_grad, gain_two_grad]).reshape(2, wa_size, shard)
    gain_rows = jnp.pad(gain_rows.transpose(1, 0, 2), ((0, 0), (0, 14), (0, width - shard)))
    late_own = lax.psum_scatter(
        jnp.concatenate(
            [grad_qkv.astype(BF16).reshape(wa_size, -1, width), gain_rows.astype(BF16)], axis=1
        ),
        "wa",
        scatter_dimension=0,
    )
    late = lax.psum(late_own, ("ctx", "seq")).astype(F32)
    grad_qkv_own = late[: 3 * shard].reshape(3, shard, width)
    gain_own = late[3 * shard : 3 * shard + 2, :shard]
    return (
        output,
        grad_tokens,
        gain_own[0],
        grad_qkv_own,
        grad_attn_out_own,
        gain_own[1],
        grad_ffn_in_own,
        grad_ffn_out_own,
    )


def solution(mesh):
    return jax.shard_map(
        local,
        mesh=mesh,
        in_specs=(
            P("seq", "wa", "ctx"),
            P("wa"),
            P(None, "wa", None),
            P("wa", None),
            P("wa"),
            P(None, "wa", None),
            P("wa", None),
            P("seq", "wa", "ctx"),
        ),
        out_specs=(
            P("seq", "wa", "ctx"),
            P("seq", "wa", "ctx"),
            P("wa"),
            P(None, "wa", None),
            P("wa", None),
            P("wa"),
            P(None, "wa", None),
            P("wa", None),
        ),
        check_vma=False,
    )
```
